256 devices in a mesh: member: 4 (over z_lo), spec: 64 (over z_hi, y, x, core).
Axes of the slice: x: 4, y: 4, z: 8 (z_hi: 2, z_lo: 4; z = z_hi * 4 + z_lo), core: 2. Of those that a mesh axis runs over, the one named last changes fastest.
Arguments:
- spectra: bfloat16 [8, 1280, 2, 8, 1280], P('member', 'spec'), may hold values from -0.16992188 to 0.16992188
- legendre: bfloat16 [1280, 1280, 256], P('spec'), may hold values from -0.15625 to 0.15625
- assignment: int32 [1280], replicated, may hold values from 0 to 1279, each once
- clone_counts: int32 [8], replicated, may hold values from 0 to 4, as said below
- destinations: int32 [8], replicated, may hold values from 0 to 7, each once
Outputs:
- grid: float32 [8, 8, 512, 2560], P('member', None, 'spec')
- clone_weights: float32 [8], P('member')
- cloned: bfloat16 [8, 1280, 2, 8, 1280], P('member', 'spec')
The draws below stay inside these ranges and needn't reach their ends.
Inputs may be any that keep to these rules, and one draw needn't show every extreme that they name: clone_counts sum to 8; the largest is exactly 4.
All inputs are finite; a program needn't handle non-finite values.
Results may differ from the reference program's by a relative error of at most 0.0065.
Values may be sent and summed in bfloat16 or wider, within the bound.
No kernel may reach another device: no remote copies, remote signals or barrier semaphores. Data moves between devices by JAX's collectives and lax.ppermute only.
A program may use at most 128 MiB of HBM per device.

```python
import math
import jax
import jax.numpy as jnp
from jax import lax

MW = 1280
NN = 1280
NLON = 2560
FIELDS = 8
LATS = 512
LH = 256
MEMBERS = 8
MOST = 4


def draw_clone_counts(key, part):
    key = jax.random.fold_in(key, 11)
    first_key, second_key = jax.random.split(key)
    order = jax.random.permutation(first_key, MEMBERS).astype(jnp.int32)
    picks = jax.random.randint(second_key, (MEMBERS - MOST,), 1, MEMBERS)
    others = order[picks]
    member_ids = jnp.arange(MEMBERS, dtype=jnp.int32)
    spread_counts = jnp.sum((others[:, None] == member_ids[None, :]).astype(jnp.int32), axis=0)
    leader = (member_ids == order[0]).astype(jnp.int32) * MOST
    return (spread_counts + leader).astype(jnp.int32)


def levels(key, shape, pieces, least, high):
    level = 1.0
    for dim, shards_of in pieces:
        steps = jax.random.uniform(jax.random.fold_in(jax.random.fold_in(key, 6), dim), (shards_of,), jnp.float32, least / len(pieces), high / len(pieces))
        level = level * jnp.repeat(jnp.exp(steps), shape[dim] // shards_of).reshape((-1,) + (1,) * (len(shape) - 1 - dim))
    return level


def noise(key, dims, scale, most, shards=(), kind=jnp.bfloat16):
    array = jax.random.normal(key, dims, jnp.float32) * scale
    if len(shards) > 0:
        array = levels(key, dims, shards, -0.22, 0.18) * array
    return jnp.clip(array, min=-most, max=most).astype(kind)


def setup_inputs(seed: int = 0) -> dict:
    streams_of = jax.random.split(jax.random.key(seed), 6)
    spectra = noise(streams_of[0], (MEMBERS, MW, 2, FIELDS, NN), 0.025, 0.16992188, ((0, 4), (1, 64)))
    legendre = noise(streams_of[1], (MW, NN, LH), NN ** -0.5, 0.15625, ((0, 64),))
    assignment = jax.random.permutation(streams_of[2], MW).astype(jnp.int32)
    clone_counts = draw_clone_counts(jax.random.fold_in(streams_of[5], 71), 0)
    destinations = jax.random.permutation(streams_of[4], MEMBERS).astype(jnp.int32)
    return {"spectra": spectra, "legendre": legendre, "assignment": assignment, "clone_counts": clone_counts, "destinations": destinations}


def parents(clone_counts, destinations):
    member_ids = jnp.arange(clone_counts.shape[0], dtype=jnp.int32)
    slot_of = lax.optimization_barrier(jnp.sum(jnp.where(destinations[None, :] == member_ids[:, None], member_ids[None, :], 0), axis=1)).astype(jnp.int32)
    bounds = jnp.cumsum(clone_counts).astype(jnp.int32)
    return lax.optimization_barrier(jnp.sum((bounds[None, :] <= slot_of[:, None]).astype(jnp.int32), axis=1)).astype(jnp.int32)

def triangle_mask(spectra, assignment):
    degree_ids = jnp.arange(NN, dtype=jnp.int32)
    in_triangle = degree_ids[None, :] < (MW - assignment)[:, None]
    return jnp.where(in_triangle[None, :, None, None, :], spectra, jnp.zeros((), spectra.dtype))

def legendre_member(masked_one, table_even, table_odd):
    coef_rows = masked_one.astype(jnp.float32).reshape(MW, 2 * FIELDS, NN)
    even_sum = jnp.einsum('rck,rkl->rcl', coef_rows[:, :, 0::2], table_even)
    odd_sum = jnp.einsum('rck,rkl->rcl', coef_rows[:, :, 1::2], table_odd)
    north_rows = even_sum + odd_sum
    south_rows = (even_sum - odd_sum)[:, :, ::-1]
    joined = jnp.concatenate([north_rows, south_rows], axis=2)
    return joined.astype(jnp.bfloat16).reshape(MW, 2, FIELDS, LATS)

def grid_member(fourier_one, assignment):
    values = fourier_one.astype(jnp.float32)
    real_part = jnp.zeros((FIELDS, LATS, NLON // 2 + 1), jnp.float32)
    real_part = real_part.at[:, :, assignment].set(jnp.transpose(values[:, 0], (1, 2, 0)))
    imag_part = jnp.zeros((FIELDS, LATS, NLON // 2 + 1), jnp.float32)
    imag_part = imag_part.at[:, :, assignment].set(jnp.transpose(values[:, 1], (1, 2, 0)))
    return jnp.fft.irfft(lax.complex(real_part, imag_part), n=NLON, axis=-1) * NLON

def reference(spectra, legendre, assignment, clone_counts, destinations):
    masked = triangle_mask(spectra, assignment)
    table = legendre.astype(jnp.float32)
    table_even = table[:, 0::2, :]
    table_odd = table[:, 1::2, :]

    def one_member(masked_one):
        fourier_one = legendre_member(masked_one, table_even, table_odd)
        return grid_member(fourier_one, assignment)
    grid = lax.map(one_member, masked)
    box_width = NLON // 4
    row_weight = 0.5 + jnp.arange(LATS, dtype=jnp.float32) / (LATS - 1)
    sector = lax.optimization_barrier(jnp.sum(grid[:, 0, :, :box_width], axis=2))
    scores = lax.optimization_barrier(jnp.sum(sector * row_weight[None, :], axis=1)) / math.sqrt(LATS * box_width)
    boosts = jnp.exp(scores)
    clone_weights = boosts * MEMBERS / jnp.sum(boosts)
    parent = parents(clone_counts, destinations)
    cloned = jnp.take(masked, parent, axis=0)
    return (grid, clone_weights, cloned)
```

```python
import math

import jax
import jax.numpy as jnp
from jax import lax
from jax.experimental import pallas as pl
from jax.experimental.pallas import tpu as pltpu
from jax.sharding import PartitionSpec as P

NLON = 2560
NN = 1280
HALF = NLON // 2
TILES = HALF // 256
ROWS = 20
SPEC = 64
MEM = 4
GROUP = 4
STEPS = ROWS // GROUP
KEEP = 2 * ROWS
SENT = KEEP + 8
DEPTH = SPEC * KEEP
CHUNKS = NN // 128
CAP = 152
ROUNDS = 3
SLOT = 6
FINE = 8
OFF = 16
LEN = 36
RIGHT = [(0, 1), (1, 2), (2, 3)]
LEFT = [(1, 0), (2, 1), (3, 2)]
COSINE = [(-1) ** k * math.pi ** (2 * k) / math.factorial(2 * k) for k in range(10)]
ANY = pl.BlockSpec(memory_space=pl.ANY)
SMEM = pl.BlockSpec(memory_space=pltpu.SMEM)
VMEM = pl.BlockSpec(memory_space=pltpu.VMEM)
PARAMS = pltpu.CompilerParams(vmem_limit_bytes=16 * 1024 * 1024)
LARGE = pltpu.CompilerParams(vmem_limit_bytes=56 * 1024 * 1024)


def pick(mask, codes):
    total = jnp.int32(0)
    for p, code in enumerate(codes):
        if code is not None:
            total = total + jnp.where((mask >> p) & 1 == 1, code, 0)
    return total


def plan(counts, dest, par, table):
    bounds = []
    total = jnp.int32(0)
    for s in range(8):
        total = total + counts[s]
        bounds.append(total)
    for k in range(8):
        parent = jnp.int32(0)
        for s in range(8):
            parent = parent + jnp.where(bounds[s] <= k, 1, 0)
        par[dest[k]] = parent
    one = jnp.int32(1)
    need = [(one << par[2 * d]) | (one << par[2 * d + 1]) for d in range(MEM)]
    have = [jnp.int32(3 << (2 * c)) for c in range(MEM)]
    code = [[jnp.int32(p % 2) if p // 2 == c else jnp.int32(0) for p in range(8)] for c in range(MEM)]
    for t in range(ROUNDS):
        moves = []
        for c in range(MEM - 1):
            west = (1 << (2 * (c + 1))) - 1
            for way, a, b, homes, order in (
                (0, c, c + 1, west, range(MEM - 1, c, -1)),
                (1, c + 1, c, 255 - west, range(0, c + 1)),
            ):
                open_mask = have[a] & ~have[b] & homes
                chosen = jnp.int32(0)
                for d in reversed(list(order)):
                    wanted = open_mask & need[d]
                    chosen = jnp.where(wanted != 0, wanted, chosen)
                chosen = chosen & -chosen
                moves.append((way, a, b, chosen))
        for way, a, b, chosen in moves:
            table[a, 2 * t + way] = pick(chosen, code[a])
        for way, a, b, chosen in moves:
            have[b] = have[b] | chosen
            for p in range(8):
                code[b][p] = jnp.where((chosen >> p) & 1 == 1, 2 + 2 * t + way, code[b][p])
    fine = jnp.int32(1)
    for d in range(MEM):
        fine = jnp.where(need[d] & ~have[d] == 0, fine, 0)
        for s in range(2):
            table[d, SLOT + s] = pick(one << par[2 * d + s], code[d])
    return fine


def pack_kernel(counts, dest, assignment, place, spectra, tab, own, right, left, held, packed, par, table, sems):
    fetch = pltpu.make_async_copy(spectra, held, sems.at[0])
    fetch.start()
    for c in range(MEM):
        for i in range(2 * ROUNDS):
            table[c, i] = 0
    fine = plan(counts, dest, par, table)
    for i in range(2 * ROUNDS + 2):
        tab[i] = table[place[0], i]
    tab[FINE] = fine
    total = jnp.int32(0)
    for r in range(ROWS):
        length = NN - assignment[place[1] * ROWS + r]
        tab[OFF + r] = jnp.minimum(total, CAP)
        tab[LEN + r] = length
        total = total + ((length + 127) >> 7)
    fetch.wait()

    def row(r, carry):
        start = tab[OFF + r]
        for m in range(2):
            for k in range(CHUNKS):
                packed[m, start + k] = held[m, r, :, k * 128 : (k + 1) * 128]
        return carry

    lax.fori_loop(0, ROWS, row, 0)
    copies = [
        pltpu.make_async_copy(packed.at[tab[0], pl.ds(0, CAP)], right, sems.at[1]),
        pltpu.make_async_copy(packed.at[tab[1], pl.ds(0, CAP)], left, sems.at[2]),
        pltpu.make_async_copy(packed.at[0, pl.ds(0, CAP)], own.at[0], sems.at[3]),
        pltpu.make_async_copy(packed.at[1, pl.ds(0, CAP)], own.at[1], sems.at[4]),
    ]
    for copy in copies:
        copy.start()
    for copy in copies:
        copy.wait()


def pack(counts, dest, assignment, place, spectra):
    slab = jax.ShapeDtypeStruct((CAP, 16, 128), jnp.bfloat16)
    return pl.pallas_call(
        pack_kernel,
        name="pack",
        in_specs=[SMEM, SMEM, SMEM, SMEM, ANY],
        out_specs=[SMEM, ANY, ANY, ANY],
        out_shape=[
            jax.ShapeDtypeStruct((64,), jnp.int32),
            jax.ShapeDtypeStruct((2, CAP, 16, 128), jnp.bfloat16),
            slab,
            slab,
        ],
        scratch_shapes=[
            pltpu.VMEM((2, ROWS, 16, NN), jnp.bfloat16),
            pltpu.VMEM((2, CAP + 16, 16, 128), jnp.bfloat16),
            pltpu.SMEM((8,), jnp.int32),
            pltpu.SMEM((MEM, 8), jnp.int32),
            pltpu.SemaphoreType.DMA((5,)),
        ],
        compiler_params=PARAMS,
        cost_estimate=pl.CostEstimate(flops=0, bytes_accessed=6_000_000, transcendentals=0),
    )(counts, dest, assignment, place, spectra)


def choose(code, slabs, target, sem):
    for k, slab in enumerate(slabs):

        @pl.when(code == k)
        def _():
            pltpu.make_async_copy(slab, target, sem).start()


def relay(t, way, tab, own, arrived, after):
    def kernel(*refs):
        tab_ref, own_ref = refs[0], refs[1]
        slabs = [own_ref.at[0], own_ref.at[1], *refs[2 : 2 + t]]
        out, sem = refs[-2], refs[-1]
        code = tab_ref[2 * t + way]
        for k, slab in enumerate(slabs):

            @pl.when(code == (k if k < 2 else 2 + 2 * (k - 2) + way))
            def _():
                pltpu.make_async_copy(slab, out, sem).start()

        pltpu.make_async_copy(slabs[0], out, sem).wait()

    return pl.pallas_call(
        kernel,
        name="relay%d%s" % (t, "rl"[way]),
        in_specs=[SMEM] + [ANY] * (2 + t),
        out_specs=ANY,
        out_shape=jax.ShapeDtypeStruct((CAP, 16, 128), jnp.bfloat16),
        scratch_shapes=[pltpu.SemaphoreType.DMA],
        compiler_params=PARAMS,
        cost_estimate=pl.CostEstimate(flops=0, bytes_accessed=1_300_000, transcendentals=0),
    )(tab, own, *arrived, after)


def hold_kernel(*refs):
    pass


def hold(value, *after):
    return pl.pallas_call(
        hold_kernel,
        name="hold",
        in_specs=[ANY] * (1 + len(after)),
        out_specs=ANY,
        out_shape=jax.ShapeDtypeStruct(value.shape, value.dtype),
        input_output_aliases={0: 0},
        compiler_params=PARAMS,
        cost_estimate=pl.CostEstimate(flops=30_000_000_000, bytes_accessed=0, transcendentals=0),
    )(value, *after)


def unpack_kernel(*refs):
    tab, own, *rest = refs
    slabs = [own.at[0], own.at[1], *rest[: 2 * ROUNDS]]
    out, plain, packed, sems = rest[2 * ROUNDS + 1 :]
    for s in range(2):
        choose(tab[SLOT + s], slabs, packed.at[s, pl.ds(0, CAP)], sems.at[s])
    for s in range(2):
        pltpu.make_async_copy(own.at[0], packed.at[s, pl.ds(0, CAP)], sems.at[s]).wait()
        lane = lax.broadcasted_iota(jnp.int32, (16, 128), 1)

        def row(r, carry):
            start = tab[OFF + r]
            length = tab[LEN + r]
            for k in range(CHUNKS):
                value = packed[s, start + k]
                kept = jnp.where(lane + k * 128 < length, value, jnp.zeros_like(value))
                plain[s, r, :, k * 128 : (k + 1) * 128] = kept
            return carry

        lax.fori_loop(0, ROWS, row, 0)
        pltpu.make_async_copy(plain.at[s], out.at[s], sems.at[2 + s]).start()
    for s in range(2):
        pltpu.make_async_copy(plain.at[s], out.at[s], sems.at[2 + s]).wait()


def unpack(tab, own, arrived, after):
    return pl.pallas_call(
        unpack_kernel,
        name="unpack",
        in_specs=[SMEM] + [ANY] * (2 + 2 * ROUNDS),
        out_specs=ANY,
        out_shape=pltpu.HBM((2, ROWS, 16, NN), jnp.bfloat16),
        scratch_shapes=[
            pltpu.VMEM((2, ROWS, 16, NN), jnp.bfloat16),
            pltpu.VMEM((2, CAP + 16, 16, 128), jnp.bfloat16),
            pltpu.SemaphoreType.DMA((4,)),
        ],
        compiler_params=PARAMS,
        cost_estimate=pl.CostEstimate(flops=0, bytes_accessed=3_000_000, transcendentals=0),
    )(tab, own, *arrived, after)


def swap_blocks(x):
    t = lax.broadcasted_iota(jnp.int32, x.shape, 1)
    s = lax.broadcasted_iota(jnp.int32, x.shape, 2) >> 4
    for k in (1, 2, 4):
        low_t = (t & k) == 0
        low_s = (s & k) == 0
        up = pltpu.roll(pltpu.roll(x, 8 - k, 1), 16 * k, 2)
        down = up if k == 4 else pltpu.roll(pltpu.roll(x, k, 1), 128 - 16 * k, 2)
        x = jnp.where(low_t == low_s, x, jnp.where(low_t, up, down))
    return x


def cosine(phase):
    phase = phase - NLON * jnp.floor(phase * (1.0 / NLON) + 0.5)
    part = phase * (2.0 / NLON)
    square = part * part
    total = COSINE[-1]
    for factor in COSINE[-2::-1]:
        total = total * square + factor
    return total


def sector(wave):
    a = jnp.full((8, 128), wave, jnp.int32).astype(jnp.float32)
    x = lax.broadcasted_iota(jnp.int32, (8, 128), 0) * 128 + lax.broadcasted_iota(jnp.int32, (8, 128), 1)
    phase = a * x.astype(jnp.float32)
    weight = jnp.where(a == 0.0, 1.0, 2.0) * (1.0 / math.sqrt(512 * (NLON // 4)))
    weight = jnp.where(x < NLON // 4, weight, 0.0)
    return [
        jnp.sum(jnp.sum(v * weight, axis=0, keepdims=True), axis=1, keepdims=True) for v in (cosine(phase), cosine(phase + NLON // 4))
    ]


def legendre_kernel(tab, spectra, legendre, out, blocks, sums):
    q = pl.program_id(0)
    lats = lax.broadcasted_iota(jnp.int32, (1, 256), 1).astype(jnp.float32)
    north = 0.5 + lats * (1.0 / 511.0)
    south = 0.5 + (511.0 - lats) * (1.0 / 511.0)

    @pl.when(q == 0)
    def _():
        sums[...] = jnp.zeros_like(sums)

    lane = lax.broadcasted_iota(jnp.int32, (32, NN), 1)
    odd = (lane & 1) == 1
    sides = [[None] * 16, [None] * 16]
    totals = [sums[0:1, :], sums[1:2, :]]
    for r in range(GROUP):
        length = tab[LEN + q * GROUP + r]
        factors = sector(NN - length)
        x = spectra[:, r].reshape(32, NN)
        x = jnp.where(lane < length, x, jnp.zeros_like(x))
        signed = jnp.where(odd, -x, x)
        both = jnp.concatenate([x, signed], axis=0)
        got = jnp.dot(both, legendre[r], preferred_element_type=jnp.float32)
        for c in range(2):
            for i in range(2):
                at = i * 16 + c * 8
                for side in range(2):
                    sides[side][(c * GROUP + r) * 2 + i] = got[side * 32 + at : side * 32 + at + 8]
                up, down = (
                    got[k : k + 1].astype(jnp.bfloat16).astype(jnp.float32) for k in (at, 32 + at)
                )
                totals[i] = totals[i] + factors[c] * (up * north + down * south)
    sums[0:1, :] = totals[0]
    sums[1:2, :] = totals[1]
    rows = pl.ds(pl.multiple_of(q * 8, 8), 8)
    upper = swap_blocks(jnp.concatenate(sides[0], axis=0).T.reshape(32, 8, 128))
    blocks[0:32, rows, :] = upper
    lower = swap_blocks(jnp.concatenate(sides[1], axis=0).T.reshape(32, 8, 128))
    for b in range(32):
        blocks[63 - b, rows, :] = lower[b]

    @pl.when(q == STEPS - 1)
    def _():
        at = lax.broadcasted_iota(jnp.int32, (8, 128), 0)
        parts = jnp.zeros((8, 128), jnp.float32)
        for i in range(2):
            left = jnp.sum(totals[i], axis=1, keepdims=True)
            for k in range(3):
                part = left.astype(jnp.bfloat16).astype(jnp.float32)
                left = left - part
                parts = jnp.where(at == 2 * k + i, part, parts)
        blocks[:, KEEP:SENT, :] = jnp.broadcast_to(parts[None], (SPEC, 8, 128))
        out[...] = blocks[...].astype(jnp.bfloat16)


def legendre_sums(tab, spectra, legendre):
    return pl.pallas_call(
        legendre_kernel,
        name="legendre",
        grid=(STEPS,),
        in_specs=[
            SMEM,
            pl.BlockSpec((2, GROUP, 16, NN), lambda q: (0, q, 0, 0)),
            pl.BlockSpec((GROUP, NN, 256), lambda q: (q, 0, 0)),
        ],
        out_specs=pl.BlockSpec((SPEC, SENT, 128), lambda q: (0, 0, 0)),
        out_shape=jax.ShapeDtypeStruct((SPEC, SENT, 128), jnp.bfloat16),
        scratch_shapes=[
            pltpu.VMEM((SPEC, SENT, 128), jnp.float32),
            pltpu.VMEM((2, 256), jnp.float32),
        ],
        compiler_params=LARGE,
        cost_estimate=pl.CostEstimate(flops=900_000_000, bytes_accessed=16_000_000, transcendentals=0),
    )(tab, spectra, legendre)


def table_kernel(tab, waves, after, out, sign, fast, counted, held, sems):
    step = pl.program_id(0)
    slot = step & 1
    own = waves[pl.ds(step, 1), :]
    high = jnp.floor(own * (1.0 / 64))
    k = lax.broadcasted_iota(jnp.int32, (256, 128), 0)
    n = lax.broadcasted_iota(jnp.int32, (256, 128), 1)
    spread = ((k >> 3) * 4 + (k & 3) == n).astype(jnp.float32).astype(jnp.bfloat16)

    def column(row):
        rows = jnp.broadcast_to(row, (128, 128)).astype(jnp.bfloat16)
        return lax.dot_general(spread, rows, (((1,), (1,)), ((), ())), preferred_element_type=jnp.float32)

    a = 64.0 * column(high) + column(own - 64.0 * high)
    parity = own - 2.0 * jnp.floor(own * 0.5)
    signs = jnp.broadcast_to(1.0 - 2.0 * parity, (8, 128)).astype(jnp.bfloat16)
    sign[...] = lax.dot_general(signs, spread, (((1,), (1,)), ((), ())), preferred_element_type=jnp.float32)

    @pl.when(step == 0)
    def _():
        counted[...] = jnp.zeros_like(counted)

    chunks = jnp.floor((NN + 127.0 - own) * (1.0 / 128))
    place = lax.broadcasted_iota(jnp.int32, (128, 128), 0) + step * 128
    first = lax.broadcasted_iota(jnp.int32, (128, 128), 1) * ROWS
    within = ((place >= first) & (place < first + ROWS)).astype(jnp.float32).astype(jnp.bfloat16)
    counted[...] += jnp.dot(
        jnp.broadcast_to(chunks, (8, 128)).astype(jnp.bfloat16), within, preferred_element_type=jnp.float32
    )

    def store(at):
        rows = pl.ds(pl.multiple_of(at * 256, 256), 256)
        return pltpu.make_async_copy(held.at[at & 1], out.at[:, rows, :], sems.at[at & 1])

    @pl.when(step >= 2)
    def _():
        store(step - 2).wait()

    piece = 64
    lane = n[:piece].astype(jnp.float32)
    part = ((k[:piece] >> 2) & 1).astype(jnp.float32) * (NLON // 4)
    for i in range(0, 256, piece):
        wave = a[i : i + piece]
        weight = jnp.where(wave == 0.0, 1.0, 2.0)
        turn = wave * 128.0
        phase = wave * lane + part
        now = cosine(phase) * weight
        later = cosine(phase + turn) * weight
        twice = 2.0 * cosine(turn)
        for j in range(HALF // 128):
            at = (j % 2) * 128
            held[slot, j // 2, i : i + piece, at : at + 128] = now.astype(jnp.bfloat16)
            now, later = later, twice * later - now

    store(step).start()

    @pl.when(step == DEPTH // 256 - 1)
    def _():
        most = jnp.max(counted[...]).astype(jnp.int32)
        fast[0] = jnp.where((most <= CAP) & (tab[FINE] == 1), 1, 0)
        store(step - 1).wait()
        store(step).wait()


def make_table(tab, waves, after):
    block = 256
    return pl.pallas_call(
        table_kernel,
        name="table",
        grid=(DEPTH // block,),
        in_specs=[SMEM, pl.BlockSpec((10, 128), lambda i: (0, 0)), ANY],
        out_specs=[
            ANY,
            pl.BlockSpec((8, block), lambda i: (0, i)),
            SMEM,
        ],
        out_shape=[
            pltpu.HBM((TILES, DEPTH, 256), jnp.bfloat16),
            jax.ShapeDtypeStruct((8, DEPTH), jnp.float32),
            jax.ShapeDtypeStruct((1,), jnp.int32),
        ],
        scratch_shapes=[
            pltpu.VMEM((8, 128), jnp.float32),
            pltpu.VMEM((2, TILES, block, 256), jnp.bfloat16),
            pltpu.SemaphoreType.DMA((2,)),
        ],
        compiler_params=PARAMS,
        cost_estimate=pl.CostEstimate(flops=60_000_000_000, bytes_accessed=8_000_000, transcendentals=0),
    )(tab, waves, after)


def grid_kernel(south, blocks, sign, table, out, boosts, arrived, held, stacked, result, sems):
    first = pltpu.make_async_copy(blocks, arrived, sems.at[0])
    first.start()
    tiles = [pltpu.make_async_copy(table.at[j], held.at[j], sems.at[1 + j]) for j in range(TILES)]
    for tile in tiles:
        tile.start()
    first.wait()
    rows = arrived[...].astype(jnp.float32)[:, :KEEP, :].reshape(DEPTH, 128).astype(jnp.bfloat16)
    to = lax.broadcasted_iota(jnp.int32, (128, 128), 0)
    by = lax.broadcasted_iota(jnp.int32, (128, 128), 1)
    lat = jnp.where(south[0] == 1, 7 - (to & 7), to & 7)
    order = (by == lat * 16 + (to >> 3)).astype(jnp.float32).astype(jnp.bfloat16)
    turned = lax.dot_general(order, rows, (((1,), (1,)), ((), ())), preferred_element_type=jnp.float32)
    stacked[0:128, :] = turned.astype(jnp.bfloat16)
    stacked[128:256, :] = (turned * sign[0:1, :]).astype(jnp.bfloat16)
    parts = jnp.sum(arrived[:, KEEP:SENT, :].astype(jnp.float32), axis=0)
    values = jnp.exp(parts[0:2] + parts[2:4] + parts[4:6])
    boosts[...] = jnp.concatenate([values, values, values[0:1] + values[1:2], jnp.zeros((3, 128))], axis=0)
    stores = []
    for j in range(TILES):
        tiles[j].wait()
        got = jnp.dot(stacked[...], held[j], preferred_element_type=jnp.float32)
        for half in range(2):
            at = pl.ds(half * HALF + j * 256, 256)
            result[:, at] = got[half * 128 : half * 128 + 128]
            stores.append(pltpu.make_async_copy(result.at[:, at], out.at[:, at], sems.at[1 + TILES + 2 * j + half]))
            stores[-1].start()
    for store in stores:
        store.wait()


def make_grid(south, blocks, sign, table):
    return pl.pallas_call(
        grid_kernel,
        name="dft",
        in_specs=[SMEM, ANY, VMEM, ANY],
        out_specs=[ANY, VMEM],
        out_shape=[
            pltpu.HBM((128, NLON), jnp.float32),
            jax.ShapeDtypeStruct((8, 128), jnp.float32),
        ],
        scratch_shapes=[
            pltpu.VMEM((SPEC, SENT, 128), jnp.bfloat16),
            pltpu.VMEM((TILES, DEPTH, 256), jnp.bfloat16),
            pltpu.VMEM((256, DEPTH), jnp.bfloat16),
            pltpu.VMEM((128, NLON), jnp.float32),
            pltpu.SemaphoreType.DMA((1 + 3 * TILES,)),
        ],
        compiler_params=LARGE,
        cost_estimate=pl.CostEstimate(flops=60_000_000_000, bytes_accessed=9_000_000, transcendentals=0),
    )(south, blocks, sign, table)


def on_device(spectra, legendre, assignment, clone_counts, destinations):
    spec_idx = lax.axis_index("spec")
    member_idx = lax.axis_index("member")
    rows = spectra.reshape(2, ROWS, 16, NN)

    place = jnp.stack([member_idx, spec_idx]).astype(jnp.int32)
    tab, own, right, left = pack(clone_counts, destinations, assignment, place, rows)
    rights = [lax.ppermute(right, "member", RIGHT)]
    lefts = [lax.ppermute(left, "member", LEFT)]
    sent = legendre_sums(tab, rows, legendre)

    right = relay(1, 0, tab, own, rights, sent)
    rights.append(lax.ppermute(right, "member", RIGHT))
    left = relay(1, 1, tab, own, lefts, right)
    lefts.append(lax.ppermute(left, "member", LEFT))
    blocks = lax.all_to_all(hold(sent, right, left), "spec", split_axis=0, concat_axis=0, tiled=True)

    right = relay(2, 0, tab, own, rights, left)
    rights.append(lax.ppermute(right, "member", RIGHT))
    left = relay(2, 1, tab, own, lefts, right)
    lefts.append(lax.ppermute(left, "member", LEFT))
    arrived = [slab for pair in zip(rights, lefts) for slab in pair]

    table, sign, fast = make_table(tab, assignment.astype(jnp.float32).reshape(10, 128), left)
    south = (spec_idx >= SPEC // 2).astype(jnp.int32).reshape(1)
    flat, boosts = make_grid(south, blocks, sign, table)
    grid = flat.reshape(2, 8, 8, NLON)
    total = boosts
    for o in range(1, MEM):
        total = total + lax.ppermute(boosts, "member", [(s, (s + o) % MEM) for s in range(MEM)])
    weights = boosts[0:2, 0] * 8.0 / total[4, 0]

    def general():
        wave = lax.dynamic_slice_in_dim(assignment, spec_idx * ROWS, ROWS)
        inside = jnp.arange(NN, dtype=jnp.int32)[None, :] < (NN - wave)[:, None]
        masked = jnp.where(inside[None, :, None, :], rows, jnp.zeros((), rows.dtype))
        bounds = jnp.cumsum(clone_counts)
        ids = jnp.arange(8, dtype=jnp.int32)
        slot = jnp.sum(jnp.where(destinations[None, :] == ids[:, None], ids[None, :], 0), axis=1)
        parent = jnp.sum((bounds[None, :] <= slot[:, None]).astype(jnp.int32), axis=1)
        mine_now = lax.dynamic_slice_in_dim(parent, member_idx * 2, 2)
        cloned = jnp.zeros_like(rows)
        for o in range(MEM):
            block = masked
            if o > 0:
                block = lax.ppermute(masked, "member", [(s, (s + o) % MEM) for s in range(MEM)])
            home = (member_idx - o) % MEM
            for i in range(2):
                cloned = jnp.where((mine_now == home * 2 + i)[:, None, None, None], block[i][None], cloned)
        return cloned

    cloned = lax.cond(fast[0] == 1, lambda: unpack(tab, own, arrived, flat), general)
    return grid, weights, cloned.reshape(2, ROWS, 2, 8, NN)


def solution(mesh):
    placed = (P("member", "spec", None, None, None), P("spec", None, None), P(), P(), P())
    return jax.shard_map(
        on_device,
        mesh=mesh,
        in_specs=placed,
        out_specs=(
            P("member", None, "spec", None),
            P("member"),
            P("member", "spec", None, None, None),
        ),
        check_vma=False,
    )
```

```python
import functools
import math

import jax
import jax.numpy as jnp
from jax import lax
from jax.experimental import pallas as pl
from jax.experimental.pallas import tpu as pltpu
from jax.sharding import PartitionSpec as P

NLON = 2560
NN = 1280
QUARTER = NLON // 4
BLOCK = 512
ROWS = 20
SPEC = 64
MEM = 4
GROUP = 4
STEPS = ROWS // GROUP
KEEP = 2 * ROWS
SENT = KEEP + 8
DEPTH = SPEC * KEEP
CHUNKS = NN // 128
CAP = 152
ROUNDS = 4
SLOT = 2 * ROUNDS
FINE = 10
MORE = 11
OFF = 16
LEN = 36
RIGHT = [(0, 1), (1, 2), (2, 3)]
LEFT = [(1, 0), (2, 1), (3, 2)]
COSINE = [(-1) ** k * math.pi ** (2 * k) / math.factorial(2 * k) for k in range(9)]
ANY = pl.BlockSpec(memory_space=pl.ANY)
SMEM = pl.BlockSpec(memory_space=pltpu.SMEM)
VMEM = pl.BlockSpec(memory_space=pltpu.VMEM)
PARAMS = pltpu.CompilerParams(vmem_limit_bytes=16 * 1024 * 1024)
LARGE = pltpu.CompilerParams(vmem_limit_bytes=56 * 1024 * 1024)


def pick(mask, codes):
    total = jnp.int32(0)
    for p, code in enumerate(codes):
        if code is not None:
            total = total + jnp.where((mask >> p) & 1 == 1, code, 0)
    return total


def plan(counts, dest, par, table):
    bounds = []
    total = jnp.int32(0)
    for s in range(8):
        total = total + counts[s]
        bounds.append(total)
    for k in range(8):
        parent = jnp.int32(0)
        for s in range(8):
            parent = parent + jnp.where(bounds[s] <= k, 1, 0)
        par[dest[k]] = parent
    one = jnp.int32(1)
    need = [(one << par[2 * d]) | (one << par[2 * d + 1]) for d in range(MEM)]
    have = [jnp.int32(3 << (2 * c)) for c in range(MEM)]
    code = [[jnp.int32(p % 2) if p // 2 == c else jnp.int32(0) for p in range(8)] for c in range(MEM)]
    for t in range(ROUNDS):
        moves = []
        for c in range(MEM - 1):
            west = (1 << (2 * (c + 1))) - 1
            for way, a, b, homes, order in (
                (0, c, c + 1, west, range(MEM - 1, c, -1)),
                (1, c + 1, c, 255 - west, range(0, c + 1)),
            ):
                open_mask = have[a] & ~have[b] & homes
                chosen = jnp.int32(0)
                for d in reversed(list(order)):
                    wanted = open_mask & need[d]
                    chosen = jnp.where(wanted != 0, wanted, chosen)
                chosen = chosen & -chosen
                moves.append((way, a, b, chosen))
        for way, a, b, chosen in moves:
            table[a, 2 * t + way] = pick(chosen, code[a])
        if t == ROUNDS - 1:
            more = functools.reduce(lambda x, y: x | y, [move[3] for move in moves])
        for way, a, b, chosen in moves:
            have[b] = have[b] | chosen
            for p in range(8):
                code[b][p] = jnp.where((chosen >> p) & 1 == 1, 2 + 2 * t + way, code[b][p])
    fine = jnp.int32(1)
    for d in range(MEM):
        fine = jnp.where(need[d] & ~have[d] == 0, fine, 0)
        for s in range(2):
            table[d, SLOT + s] = pick(one << par[2 * d + s], code[d])
    return fine, more


def pack_kernel(counts, dest, assignment, place, spectra, tab, own, right, left, held, packed, par, table, sems):
    fetches = [pltpu.make_async_copy(spectra.at[m], held.at[m], sems.at[m]) for m in range(2)]
    for fetch in fetches:
        fetch.start()
    for c in range(MEM):
        for i in range(2 * ROUNDS):
            table[c, i] = 0
    fine, more = plan(counts, dest, par, table)
    for i in range(2 * ROUNDS + 2):
        tab[i] = table[place[0], i]
    tab[FINE] = fine
    tab[MORE] = more
    total = jnp.int32(0)
    for r in range(ROWS):
        length = NN - assignment[place[1] * ROWS + r]
        tab[OFF + r] = jnp.minimum(total, CAP)
        tab[LEN + r] = length
        total = total + ((length + 127) >> 7)
    sends = ((right, tab[0], 2), (left, tab[1], 3))
    keeps = []
    for m in range(2):
        fetches[m].wait()

        def row(r, carry):
            start = tab[OFF + r]
            for k in range(CHUNKS):
                packed[m, start + k] = held[m, r, :, k * 128 : (k + 1) * 128]
            return carry

        lax.fori_loop(0, ROWS, row, 0)
        slab = packed.at[m, pl.ds(0, CAP)]
        for target, code, sem in sends:

            @pl.when(code == m)
            def _():
                pltpu.make_async_copy(slab, target, sems.at[sem]).start()

        keeps.append(pltpu.make_async_copy(slab, own.at[m], sems.at[4 + m]))
        keeps[m].start()
    for target, code, sem in sends:
        pltpu.make_async_copy(packed.at[0, pl.ds(0, CAP)], target, sems.at[sem]).wait()
    for keep in keeps:
        keep.wait()


def pack(counts, dest, assignment, place, spectra):
    slab = jax.ShapeDtypeStruct((CAP, 16, 128), jnp.bfloat16)
    return pl.pallas_call(
        pack_kernel,
        name="pack",
        in_specs=[SMEM, SMEM, SMEM, SMEM, ANY],
        out_specs=[SMEM, ANY, ANY, ANY],
        out_shape=[
            jax.ShapeDtypeStruct((64,), jnp.int32),
            jax.ShapeDtypeStruct((2, CAP, 16, 128), jnp.bfloat16),
            slab,
            slab,
        ],
        scratch_shapes=[
            pltpu.VMEM((2, ROWS, 16, NN), jnp.bfloat16),
            pltpu.VMEM((2, CAP + 16, 16, 128), jnp.bfloat16),
            pltpu.SMEM((8,), jnp.int32),
            pltpu.SMEM((MEM, 16), jnp.int32),
            pltpu.SemaphoreType.DMA((6,)),
        ],
        compiler_params=PARAMS,
        cost_estimate=pl.CostEstimate(flops=0, bytes_accessed=6_000_000, transcendentals=0),
    )(counts, dest, assignment, place, spectra)


def relay(t, way, tab, own, arrived, after):
    def kernel(*refs):
        tab_ref, own_ref = refs[0], refs[1]
        slabs = [own_ref.at[0], own_ref.at[1], *refs[2 : 2 + t]]
        out, sem = refs[-2], refs[-1]
        code = tab_ref[2 * t + way]
        for k, slab in enumerate(slabs):

            @pl.when(code == (k if k < 2 else 2 + 2 * (k - 2) + way))
            def _():
                pltpu.make_async_copy(slab, out, sem).start()

        pltpu.make_async_copy(slabs[0], out, sem).wait()

    return pl.pallas_call(
        kernel,
        name="relay%d%s" % (t, "rl"[way]),
        in_specs=[SMEM] + [ANY] * (2 + t),
        out_specs=ANY,
        out_shape=jax.ShapeDtypeStruct((CAP, 16, 128), jnp.bfloat16),
        scratch_shapes=[pltpu.SemaphoreType.DMA],
        compiler_params=PARAMS,
        cost_estimate=pl.CostEstimate(flops=0, bytes_accessed=1_300_000, transcendentals=0),
    )(tab, own, *arrived, after)


def hold_kernel(*refs):
    pass


def hold(value, *after):
    return pl.pallas_call(
        hold_kernel,
        name="hold",
        in_specs=[ANY] * (1 + len(after)),
        out_specs=ANY,
        out_shape=jax.ShapeDtypeStruct(value.shape, value.dtype),
        input_output_aliases={0: 0},
        compiler_params=PARAMS,
        cost_estimate=pl.CostEstimate(flops=30_000_000_000, bytes_accessed=0, transcendentals=0),
    )(value, *after)


def unpack(tab, own, arrived, flat, weights):
    codes = sorted(arrived)

    def kernel(*refs):
        tab, own = refs[:2]
        out, plain, packed, sems = refs[-4:]
        slabs = {0: own.at[0], 1: own.at[1], **dict(zip(codes, refs[2:]))}
        for s in range(2):
            for code, slab in slabs.items():

                @pl.when(tab[SLOT + s] == code)
                def _():
                    pltpu.make_async_copy(slab, packed.at[s, pl.ds(0, CAP)], sems.at[s]).start()

        lane = lax.broadcasted_iota(jnp.int32, (16, 128), 1)
        for s in range(2):
            pltpu.make_async_copy(own.at[0], packed.at[s, pl.ds(0, CAP)], sems.at[s]).wait()

            def row(r, carry):
                start = tab[OFF + r]
                length = tab[LEN + r]
                for k in range(CHUNKS):
                    value = packed[s, start + k]
                    kept = jnp.where(lane + k * 128 < length, value, jnp.zeros_like(value))
                    plain[s, r, :, k * 128 : (k + 1) * 128] = kept
                return carry

            for first in range(0, ROWS, 5):
                lax.fori_loop(first, first + 5, row, 0)
                rows = pl.ds(first, 5)
                pltpu.make_async_copy(plain.at[s, rows], out.at[s, rows], sems.at[2 + s]).start()
        for s in range(2):
            pltpu.make_async_copy(plain.at[s], out.at[s], sems.at[2 + s]).wait()

    return pl.pallas_call(
        kernel,
        name="unpack",
        in_specs=[SMEM] + [ANY] * (2 + len(codes)) + [SMEM],
        out_specs=ANY,
        out_shape=pltpu.HBM((2, ROWS, 16, NN), jnp.bfloat16),
        scratch_shapes=[
            pltpu.VMEM((2, ROWS, 16, NN), jnp.bfloat16),
            pltpu.VMEM((2, CAP + 16, 16, 128), jnp.bfloat16),
            pltpu.SemaphoreType.DMA((4,)),
        ],
        compiler_params=PARAMS,
        cost_estimate=pl.CostEstimate(flops=0, bytes_accessed=3_000_000, transcendentals=0),
    )(tab, own, *[arrived[code] for code in codes], flat, weights)


def swap_blocks(x):
    t = lax.broadcasted_iota(jnp.int32, x.shape, 1)
    s = lax.broadcasted_iota(jnp.int32, x.shape, 2) >> 4
    for k in (1, 2, 4):
        low_t = (t & k) == 0
        low_s = (s & k) == 0
        up = pltpu.roll(pltpu.roll(x, 8 - k, 1), 16 * k, 2)
        down = up if k == 4 else pltpu.roll(pltpu.roll(x, k, 1), 128 - 16 * k, 2)
        x = jnp.where(low_t == low_s, x, jnp.where(low_t, up, down))
    return x


def cosine(phase):
    phase = phase - NLON * jnp.floor(phase * (1.0 / NLON) + 0.5)
    part = phase * (2.0 / NLON)
    square = part * part
    total = COSINE[-1]
    for factor in COSINE[-2::-1]:
        total = total * square + factor
    return total


def sector(wave):
    a = jnp.full((8, 128), wave, jnp.int32).astype(jnp.float32)
    x = lax.broadcasted_iota(jnp.int32, (8, 128), 0) * 128 + lax.broadcasted_iota(jnp.int32, (8, 128), 1)
    phase = a * x.astype(jnp.float32)
    weight = jnp.where(a == 0.0, 1.0, 2.0) * (1.0 / math.sqrt(512 * (QUARTER)))
    weight = jnp.where(x < QUARTER, weight, 0.0)
    return [
        jnp.sum(jnp.sum(v * weight, axis=0, keepdims=True), axis=1, keepdims=True) for v in (cosine(phase), cosine(phase + QUARTER))
    ]


def legendre_kernel(tab, spectra, legendre, out, blocks, sums):
    q = pl.program_id(0)
    lats = lax.broadcasted_iota(jnp.int32, (1, 256), 1).astype(jnp.float32)
    north = 0.5 + lats * (1.0 / 511.0)
    south = 0.5 + (511.0 - lats) * (1.0 / 511.0)

    @pl.when(q == 0)
    def _():
        sums[...] = jnp.zeros_like(sums)

    lane = lax.broadcasted_iota(jnp.int32, (32, NN), 1)
    odd = (lane & 1) == 1
    sides = [[None] * 16, [None] * 16]
    totals = [sums[0:1, :], sums[1:2, :]]
    for r in range(GROUP):
        length = tab[LEN + q * GROUP + r]
        factors = sector(NN - length)
        x = spectra[:, r].reshape(32, NN)
        x = jnp.where(lane < length, x, jnp.zeros_like(x))
        signed = jnp.where(odd, -x, x)
        both = jnp.concatenate([x, signed], axis=0)
        got = jnp.dot(both, legendre[r], preferred_element_type=jnp.float32)
        for c in range(2):
            for i in range(2):
                at = i * 16 + c * 8
                for side in range(2):
                    sides[side][(c * GROUP + r) * 2 + i] = got[side * 32 + at : side * 32 + at + 8]
                up, down = (
                    got[k : k + 1].astype(jnp.bfloat16).astype(jnp.float32) for k in (at, 32 + at)
                )
                totals[i] = totals[i] + factors[c] * (up * north + down * south)
    sums[0:1, :] = totals[0]
    sums[1:2, :] = totals[1]
    rows = pl.ds(pl.multiple_of(q * 8, 8), 8)
    upper = swap_blocks(jnp.concatenate(sides[0], axis=0).T.reshape(32, 8, 128))
    blocks[0:32, rows, :] = upper
    lower = swap_blocks(jnp.concatenate(sides[1], axis=0).T.reshape(32, 8, 128))
    for b in range(32):
        blocks[63 - b, rows, :] = lower[b]

    @pl.when(q == STEPS - 1)
    def _():
        at = lax.broadcasted_iota(jnp.int32, (8, 128), 0)
        parts = jnp.zeros((8, 128), jnp.float32)
        for i in range(2):
            left = jnp.sum(totals[i], axis=1, keepdims=True)
            for k in range(3):
                part = left.astype(jnp.bfloat16).astype(jnp.float32)
                left = left - part
                parts = jnp.where(at == 2 * k + i, part, parts)
        blocks[:, KEEP:SENT, :] = jnp.broadcast_to(parts[None], (SPEC, 8, 128))
        out[...] = blocks[...].astype(jnp.bfloat16)


def legendre_sums(tab, spectra, legendre):
    return pl.pallas_call(
        legendre_kernel,
        name="legendre",
        grid=(STEPS,),
        in_specs=[
            SMEM,
            pl.BlockSpec((2, GROUP, 16, NN), lambda q: (0, q, 0, 0)),
            pl.BlockSpec((GROUP, NN, 256), lambda q: (q, 0, 0)),
        ],
        out_specs=pl.BlockSpec((SPEC, SENT, 128), lambda q: (0, 0, 0)),
        out_shape=jax.ShapeDtypeStruct((SPEC, SENT, 128), jnp.bfloat16),
        scratch_shapes=[
            pltpu.VMEM((SPEC, SENT, 128), jnp.float32),
            pltpu.VMEM((2, 256), jnp.float32),
        ],
        compiler_params=LARGE,
        cost_estimate=pl.CostEstimate(flops=900_000_000, bytes_accessed=16_000_000, transcendentals=0),
    )(tab, spectra, legendre)


def table_kernel(tab, waves, after, out, sign, branch, counted, held, sems):
    step = pl.program_id(0)
    slot = step & 1
    k = lax.broadcasted_iota(jnp.int32, (256, 128), 0)
    n = lax.broadcasted_iota(jnp.int32, (256, 128), 1)
    spread = ((k >> 3) * 4 + (k & 3) == n).astype(jnp.float32).astype(jnp.bfloat16)

    def column(row):
        rows = jnp.broadcast_to(row, (128, 128)).astype(jnp.bfloat16)
        return lax.dot_general(spread, rows, (((1,), (1,)), ((), ())), preferred_element_type=jnp.float32)

    @pl.when(step == 0)
    def _():
        counted[...] = jnp.zeros_like(counted)

    def store(at):
        rows = pl.ds(pl.multiple_of(at * BLOCK, BLOCK), BLOCK)
        return pltpu.make_async_copy(held.at[at & 1], out.at[rows, :], sems.at[at & 1])

    @pl.when(step >= 2)
    def _():
        store(step - 2).wait()

    columns = []
    for part in range(BLOCK // 256):
        at = step * (BLOCK // 256) + part
        own = waves[pl.ds(at, 1), :]
        high = jnp.floor(own * (1.0 / 64))
        wave = 64.0 * column(high) + column(own - 64.0 * high)
        turn = cosine(jnp.broadcast_to(own * 128.0, (8, 128)))[0:1]
        twice = jnp.zeros((256, 128), jnp.float32)
        for _ in range(3):
            piece = turn.astype(jnp.bfloat16).astype(jnp.float32)
            twice = twice + column(2.0 * piece)
            turn = turn - piece
        columns.append((wave, twice))
        left = own - 4.0 * jnp.floor(own * 0.25)
        one, two, three = (jnp.where(left == v, 1.0, 0.0) for v in (1.0, 2.0, 3.0))
        line = lax.broadcasted_iota(jnp.int32, (8, 128), 0)
        signs = jnp.where(
            line == 0, 1.0 - 2.0 * (one + three), jnp.where(line == 1, 1.0 - one - 2.0 * two - three, one - three)
        )
        turned = lax.dot_general(
            signs.astype(jnp.bfloat16), spread, (((1,), (1,)), ((), ())), preferred_element_type=jnp.float32
        )
        line = lax.broadcasted_iota(jnp.int32, (8, 256), 0)
        sine = (lax.broadcasted_iota(jnp.int32, (8, 256), 1) >> 2) & 1
        sign[:, part * 256 : (part + 1) * 256] = jnp.where((line == 2) & (sine == 0), -turned, turned)
        chunks = jnp.floor((NN + 127.0 - own) * (1.0 / 128))
        place = lax.broadcasted_iota(jnp.int32, (128, 128), 0) + at * 128
        first = lax.broadcasted_iota(jnp.int32, (128, 128), 1) * ROWS
        within = ((place >= first) & (place < first + ROWS)).astype(jnp.float32).astype(jnp.bfloat16)
        counted[...] += jnp.dot(
            jnp.broadcast_to(chunks, (8, 128)).astype(jnp.bfloat16), within, preferred_element_type=jnp.float32
        )

    lane = n[:64].astype(jnp.float32)
    part = ((k[:64] >> 2) & 1).astype(jnp.float32) * QUARTER
    for i in range(0, BLOCK, 64):
        wave, twice = (column[i % 256 : i % 256 + 64] for column in columns[i // 256])
        weight = jnp.where(wave == 0.0, 1.0, 2.0)
        phase = wave * lane + part
        now = cosine(phase) * weight
        later = cosine(phase + wave * 128.0) * weight
        for j in range(QUARTER // 128):
            held[slot, i : i + 64, j * 128 : (j + 1) * 128] = now.astype(jnp.bfloat16)
            now, later = later, twice * later - now

    store(step).start()

    @pl.when(step == DEPTH // BLOCK - 1)
    def _():
        most = jnp.max(counted[...]).astype(jnp.int32)
        branch[0] = jnp.where((most <= CAP) & (tab[FINE] == 1), jnp.where(tab[MORE] != 0, 2, 1), 0)
        store(step - 1).wait()
        store(step).wait()


def make_table(tab, waves, after):
    return pl.pallas_call(
        table_kernel,
        name="table",
        grid=(DEPTH // BLOCK,),
        in_specs=[SMEM, pl.BlockSpec((10, 128), lambda i: (0, 0)), ANY],
        out_specs=[
            ANY,
            pl.BlockSpec((8, BLOCK), lambda i: (0, i)),
            SMEM,
        ],
        out_shape=[
            pltpu.HBM((DEPTH, QUARTER), jnp.bfloat16),
            jax.ShapeDtypeStruct((8, DEPTH), jnp.float32),
            jax.ShapeDtypeStruct((1,), jnp.int32),
        ],
        scratch_shapes=[
            pltpu.VMEM((8, 128), jnp.float32),
            pltpu.VMEM((2, BLOCK, QUARTER), jnp.bfloat16),
            pltpu.SemaphoreType.DMA((2,)),
        ],
        compiler_params=PARAMS,
        cost_estimate=pl.CostEstimate(flops=60_000_000_000, bytes_accessed=8_000_000, transcendentals=0),
    )(tab, waves, after)


def boost_kernel(blocks, out, parts, sem):
    fetch = pltpu.make_async_copy(blocks.at[:, pl.ds(KEEP, 8), :], parts, sem)
    fetch.start()
    fetch.wait()
    total = jnp.sum(parts[...].astype(jnp.float32), axis=0)
    values = jnp.exp(total[0:2] + total[2:4] + total[4:6])
    out[...] = jnp.concatenate([values, values, values[0:1] + values[1:2], jnp.zeros((3, 128))], axis=0)


def make_boosts(blocks):
    return pl.pallas_call(
        boost_kernel,
        name="boosts",
        in_specs=[ANY],
        out_specs=VMEM,
        out_shape=jax.ShapeDtypeStruct((8, 128), jnp.float32),
        scratch_shapes=[pltpu.VMEM((SPEC, 8, 128), jnp.bfloat16), pltpu.SemaphoreType.DMA],
        compiler_params=PARAMS,
        cost_estimate=pl.CostEstimate(flops=0, bytes_accessed=200_000, transcendentals=0),
    )(blocks)


def weights_kernel(mine, *refs):
    out = refs[-1]
    total = mine[...]
    for other in refs[:-1]:
        total = total + other[...]
    share = mine[...] * 8.0 / jnp.broadcast_to(total[4:5], (8, 128))
    for i in range(2):
        out[i] = share[i, 0]


def make_weights(mine, others):
    return pl.pallas_call(
        weights_kernel,
        name="weights",
        in_specs=[VMEM] * (1 + len(others)),
        out_specs=SMEM,
        out_shape=jax.ShapeDtypeStruct((2,), jnp.float32),
        compiler_params=PARAMS,
    )(mine, *others)


def grid_kernel(south, blocks, sign, table, out, arrived, held, stacked, sems):
    first = pltpu.make_async_copy(blocks, arrived, sems.at[0])
    second = pltpu.make_async_copy(table, held, sems.at[1])
    first.start()
    second.start()
    to = lax.broadcasted_iota(jnp.int32, (128, 128), 0)
    by = lax.broadcasted_iota(jnp.int32, (128, 128), 1)
    lat = jnp.where(south[0] == 1, 7 - (to & 7), to & 7)
    order = (by == lat * 16 + (to >> 3)).astype(jnp.float32).astype(jnp.bfloat16)
    first.wait()
    rows = arrived[...].astype(jnp.float32)[:, :KEEP, :].reshape(DEPTH, 128).astype(jnp.bfloat16)
    turned = lax.dot_general(order, rows, (((1,), (1,)), ((), ())), preferred_element_type=jnp.float32)
    lane = lax.broadcasted_iota(jnp.int32, (128, 128), 1)
    for k in range(0, DEPTH, 128):
        x = turned[:, k : k + 128]
        other = jnp.where((lane & 4) == 0, pltpu.roll(x, 124, 1), pltpu.roll(x, 4, 1))
        same = x * sign[1:2, k : k + 128]
        cross = other * sign[2:3, k : k + 128]
        stacked[0:128, k : k + 128] = x.astype(jnp.bfloat16)
        stacked[128:256, k : k + 128] = (same + cross).astype(jnp.bfloat16)
        stacked[256:384, k : k + 128] = (x * sign[0:1, k : k + 128]).astype(jnp.bfloat16)
        stacked[384:512, k : k + 128] = (same - cross).astype(jnp.bfloat16)
    second.wait()
    got = jnp.dot(stacked[...], held[...], preferred_element_type=jnp.float32)
    for q in range(4):
        out[:, q * QUARTER : (q + 1) * QUARTER] = got[q * 128 : (q + 1) * 128]


def make_grid(south, blocks, sign, table):
    return pl.pallas_call(
        grid_kernel,
        name="dft",
        in_specs=[SMEM, ANY, VMEM, ANY],
        out_specs=VMEM,
        out_shape=pltpu.HBM((128, NLON), jnp.float32),
        scratch_shapes=[
            pltpu.VMEM((SPEC, SENT, 128), jnp.bfloat16),
            pltpu.VMEM((DEPTH, QUARTER), jnp.bfloat16),
            pltpu.VMEM((512, DEPTH), jnp.bfloat16),
            pltpu.SemaphoreType.DMA((2,)),
        ],
        compiler_params=LARGE,
        cost_estimate=pl.CostEstimate(flops=60_000_000_000, bytes_accessed=9_000_000, transcendentals=0),
    )(south, blocks, sign, table)


def on_device(spectra, legendre, assignment, clone_counts, destinations):
    spec_idx = lax.axis_index("spec")
    member_idx = lax.axis_index("member")
    rows = spectra.reshape(2, ROWS, 16, NN)

    place = jnp.stack([member_idx, spec_idx]).astype(jnp.int32)
    tab, own, right, left = pack(clone_counts, destinations, assignment, place, rows)
    def general():
        wave = lax.dynamic_slice_in_dim(assignment, spec_idx * ROWS, ROWS)
        inside = jnp.arange(NN, dtype=jnp.int32)[None, :] < (NN - wave)[:, None]
        masked = jnp.where(inside[None, :, None, :], rows, jnp.zeros((), rows.dtype))
        bounds = jnp.cumsum(clone_counts)
        ids = jnp.arange(8, dtype=jnp.int32)
        slot = jnp.sum(jnp.where(destinations[None, :] == ids[:, None], ids[None, :], 0), axis=1)
        parent = jnp.sum((bounds[None, :] <= slot[:, None]).astype(jnp.int32), axis=1)
        mine_now = lax.dynamic_slice_in_dim(parent, member_idx * 2, 2)
        cloned = jnp.zeros_like(rows)
        for o in range(MEM):
            block = masked
            if o > 0:
                block = lax.ppermute(masked, "member", [(s, (s + o) % MEM) for s in range(MEM)])
            home = (member_idx - o) % MEM
            for i in range(2):
                cloned = jnp.where((mine_now == home * 2 + i)[:, None, None, None], block[i][None], cloned)
        return cloned

    sends = [right, left]
    seen = [[], []]
    arrived = {}

    def start(t, way):
        got = lax.ppermute(sends[way], "member", (RIGHT, LEFT)[way])
        seen[way].append(got)
        arrived[2 + 2 * t + way] = got

    for way in range(2):
        start(0, way)
    sent = last = legendre_sums(tab, rows, legendre)
    for t in range(1, ROUNDS - 1):
        for way in range(2):
            sends[way] = last = relay(t, way, tab, own, seen[way], last)
            start(t, way)
        if t == 1:
            blocks = lax.all_to_all(hold(sent, *sends), "spec", split_axis=0, concat_axis=0, tiled=True)
            table, sign, branch = make_table(tab, assignment.astype(jnp.float32).reshape(10, 128), last)
            last = sign
    south = (spec_idx >= SPEC // 2).astype(jnp.int32).reshape(1)
    boosts = make_boosts(blocks)
    others = [lax.ppermute(boosts, "member", [(s, (s + o) % MEM) for s in range(MEM)]) for o in range(1, MEM)]
    flat = make_grid(south, blocks, sign, table)
    weights = make_weights(boosts, others)

    def one_more():
        slabs = dict(arrived)
        for way in range(2):
            last_send = relay(ROUNDS - 1, way, tab, own, seen[way], own)
            slabs[2 * ROUNDS + way] = lax.ppermute(last_send, "member", (RIGHT, LEFT)[way])
        return unpack(tab, own, slabs, flat, weights)

    cloned = lax.switch(branch[0], [general, lambda: unpack(tab, own, arrived, flat, weights), one_more])
    return flat.reshape(2, 8, 8, NLON), weights, cloned.reshape(2, ROWS, 2, 8, NN)


def solution(mesh):
    placed = (P("member", "spec", None, None, None), P("spec", None, None), P(), P(), P())
    return jax.shard_map(
        on_device,
        mesh=mesh,
        in_specs=placed,
        out_specs=(
            P("member", None, "spec", None),
            P("member"),
            P("member", "spec", None, None, None),
        ),
        check_vma=False,
    )
```
